128 devices in a mesh: grp: 32 (over z, x_hi, y), tp: 4 (over x_lo, core).
Axes of the slice: x: 4 (x_hi: 2, x_lo: 2; x = x_hi * 2 + x_lo), y: 4, z: 4, core: 2. Of those that a mesh axis runs over, the one named last changes fastest.
Arguments:
- states: bfloat16 [32768, 5120], P(('grp', 'tp')), may hold values from -27 to 27
- norm_gain: float32 [5120], replicated, may hold values from 0.5 to 1.5
- query_gain: float32 [128], replicated, may hold values from 0.1 to 1.9
- key_norm_gain: float32 [128], replicated, may hold values from 0.1 to 1.9
- lengths: int32 [1024], P('grp'), may hold values from 8 to 32
- w_query: bfloat16 [5120, 4096], P('grp', 'tp'), may hold values from -0.078125 to 0.078125
- key_weight: bfloat16 [5120, 512], P('grp', 'tp'), may hold values from -0.078125 to 0.078125
- value_weight: bfloat16 [5120, 512], P('grp', 'tp'), may hold values from -0.078125 to 0.078125
- w_out: bfloat16 [5120, 4096], P('grp', 'tp'), may hold values from -0.09375 to 0.09375
Outputs:
- attention_out: bfloat16 [32768, 5120], P(('grp', 'tp'))
The draws below stay inside these ranges and needn't reach their ends.
All inputs are finite; a program needn't handle non-finite values.
Results may differ from the reference program's by a relative error of at most 0.014.
Values may be sent and summed in bfloat16 or wider, within the bound.
No kernel may reach another device: no remote copies, remote signals or barrier semaphores. Data moves between devices by JAX's collectives and lax.ppermute only.
A program may use at most 128 MiB of HBM per device.

```python
import math
import jax
import jax.numpy as jnp
from jax import lax

MODEL_WIDTH = 5120
QUERY_HEADS = 32
KEY_VALUE_HEADS = 4
HEAD_SIZE = 128
PROMPT_LENGTH = 32
GROUP_PROMPTS = 32
TOK_GRP = 1024
TOKENS = 32768
PROMPTS = 1024
N_GRP = 32
N_TP = 4


def draw_states(key, part):
    key = jax.random.fold_in(key, 7)
    base_key, row_key, col_key = jax.random.split(key, 3)
    row_scale = jnp.exp(jax.random.uniform(row_key, (TOKENS, 1), jnp.float32, math.log(0.3), math.log(3.0)))
    col_scale = jnp.exp(jax.random.uniform(col_key, (1, MODEL_WIDTH), jnp.float32, math.log(0.3), math.log(3.0)))
    base_noise = jnp.clip(jax.random.normal(base_key, (TOKENS, MODEL_WIDTH), jnp.float32), -3.0, 3.0)
    return (base_noise * row_scale * col_scale).astype(jnp.bfloat16)


def plant(entries, stream_key, least, high):
    dims = entries.shape
    index_at = [jax.random.randint(jax.random.fold_in(stream_key, axis), (), 0, dims[axis]) for axis in range(len(dims))]
    entries = entries.at[tuple(index_at)].set(least)
    longest = dims.index(max(dims))
    index_at[longest] = (index_at[longest] + 1) % dims[longest]
    return entries.at[tuple(index_at)].set(high)


def levels(rng, extent, cuts, smallest, top_value):
    level = 1.0
    for axis_at, shards_of in cuts:
        steps = jax.random.uniform(jax.random.fold_in(jax.random.fold_in(rng, 6), axis_at), (shards_of,), jnp.float32, smallest / len(cuts), top_value / len(cuts))
        level = level * jnp.repeat(jnp.exp(steps), extent[axis_at] // shards_of).reshape((-1,) + (1,) * (len(extent) - 1 - axis_at))
    return level


def normal_values(own_key, extent, spread, reach, cuts=(), kind=jnp.bfloat16):
    values = spread * jax.random.normal(own_key, extent, jnp.float32)
    if cuts:
        values = values * levels(own_key, extent, cuts, -0.22, 0.18)
    return jnp.clip(values, -reach, reach).astype(kind)


def setup_inputs(seed: int = 0) -> dict:
    key_list = jax.random.split(jax.random.key(seed), 10)
    return {
        "states": draw_states(jax.random.fold_in(key_list[9], 71), 0),
        "norm_gain": jnp.clip(1.0 + 0.1 * jax.random.normal(key_list[1], (MODEL_WIDTH,), jnp.float32), 0.5, 1.5),
        "query_gain": jnp.clip(1.0 + 0.18 * jax.random.normal(key_list[2], (HEAD_SIZE,), jnp.float32), 0.1, 1.9),
        "key_norm_gain": jnp.clip(1.0 + 0.18 * jax.random.normal(key_list[3], (HEAD_SIZE,), jnp.float32), 0.1, 1.9),
        "lengths": plant(jax.random.randint(key_list[4], (PROMPTS,), PROMPT_LENGTH // 4, PROMPT_LENGTH + 1), jax.random.fold_in(key_list[4], 1), PROMPT_LENGTH // 4, PROMPT_LENGTH).astype(jnp.int32),
        "w_query": normal_values(key_list[5], (MODEL_WIDTH, QUERY_HEADS * HEAD_SIZE), MODEL_WIDTH ** -0.5, 0.078125, ((0, 32), (1, 4))),
        "key_weight": normal_values(key_list[6], (MODEL_WIDTH, KEY_VALUE_HEADS * HEAD_SIZE), MODEL_WIDTH ** -0.5, 0.078125, ((0, 32), (1, 4))),
        "value_weight": normal_values(key_list[7], (MODEL_WIDTH, KEY_VALUE_HEADS * HEAD_SIZE), MODEL_WIDTH ** -0.5, 0.078125, ((0, 32), (1, 4))),
        "w_out": normal_values(key_list[8], (MODEL_WIDTH, QUERY_HEADS * HEAD_SIZE), (QUERY_HEADS * HEAD_SIZE) ** -0.5, 0.09375, ((0, 32), (1, 4))),
    }


def per_head_norm(vectors, scale_gain):
    return vectors * lax.rsqrt(lax.optimization_barrier(jnp.mean(vectors * vectors, axis=-1, keepdims=True)) + 1e-06) * scale_gain

def apply_rotary(vectors):
    head_width = vectors.shape[-1]
    half_width = head_width // 2
    freq_index = jnp.arange(half_width, dtype=jnp.float32)
    frequency = jnp.exp(freq_index * (-2.0 * math.log(1000000.0) / head_width))
    positions = jnp.arange(vectors.shape[1], dtype=jnp.float32)
    angles = positions[:, None] * frequency[None, :]
    cosine_table = jnp.cos(angles)[:, None, :]
    sine_table = jnp.sin(angles)[:, None, :]
    lower_half = vectors[..., :half_width]
    upper_half = vectors[..., half_width:]
    return jnp.concatenate([lower_half * cosine_table - upper_half * sine_table, upper_half * cosine_table + lower_half * sine_table], axis=-1)

def attend(query_heads, key_heads, value_heads, group_lengths):
    head_width = query_heads.shape[-1]
    slot_length = query_heads.shape[1]
    scores = jnp.einsum('pqgrd,pkgd->pgrqk', query_heads.astype(jnp.float32), key_heads.astype(jnp.float32)) / math.sqrt(head_width)
    positions = jnp.arange(slot_length, dtype=jnp.int32)
    causal = (positions[None, :] <= positions[:, None])[None, :, :]
    live = positions[None, None, :] < group_lengths.astype(jnp.int32)[:, None, None]
    allowed = (causal & live)[:, None, None, :, :]
    weights = jnp.where(allowed, jnp.exp(scores), 0.0)
    probabilities = (weights / lax.optimization_barrier(jnp.sum(weights, axis=-1, keepdims=True))).astype(jnp.bfloat16)
    return jnp.einsum('pgrqk,pkgd->pqgrd', probabilities.astype(jnp.float32), value_heads.astype(jnp.float32)).astype(jnp.bfloat16)

def one_group(group_rows, group_lengths, norm_gain, query_gain, key_norm_gain, w_query, key_weight, value_weight, out_blocks):
    widened = group_rows.astype(jnp.float32)
    normed = (widened * lax.rsqrt(lax.optimization_barrier(jnp.mean(widened * widened, axis=-1, keepdims=True)) + 1e-06) * norm_gain).astype(jnp.bfloat16)
    queries = jnp.dot(normed, w_query, preferred_element_type=jnp.float32)
    key_token_rows = jnp.dot(normed, key_weight, preferred_element_type=jnp.float32)
    value_token_rows = jnp.dot(normed, value_weight, preferred_element_type=jnp.float32).astype(jnp.bfloat16)
    query_per_key_ratio = QUERY_HEADS // KEY_VALUE_HEADS
    query_heads = apply_rotary(per_head_norm(queries.reshape(GROUP_PROMPTS, PROMPT_LENGTH, QUERY_HEADS, HEAD_SIZE), query_gain)).astype(jnp.bfloat16)
    query_heads = query_heads.reshape(GROUP_PROMPTS, PROMPT_LENGTH, KEY_VALUE_HEADS, query_per_key_ratio, HEAD_SIZE)
    key_heads = apply_rotary(per_head_norm(key_token_rows.reshape(GROUP_PROMPTS, PROMPT_LENGTH, KEY_VALUE_HEADS, HEAD_SIZE), key_norm_gain)).astype(jnp.bfloat16)
    value_heads = value_token_rows.reshape(GROUP_PROMPTS, PROMPT_LENGTH, KEY_VALUE_HEADS, HEAD_SIZE)
    attended = attend(query_heads, key_heads, value_heads, group_lengths).reshape(TOK_GRP, QUERY_HEADS * HEAD_SIZE)
    blocks = attended.astype(jnp.float32).reshape(TOK_GRP, N_TP, QUERY_HEADS * HEAD_SIZE // N_TP)
    partials = jnp.einsum('tbc,dbc->btd', blocks, out_blocks).astype(jnp.bfloat16)
    partials = lax.optimization_barrier(partials).astype(jnp.float32)
    return lax.optimization_barrier(jnp.sum(partials, axis=0)).astype(jnp.bfloat16)

def reference(states, norm_gain, query_gain, key_norm_gain, lengths, w_query, key_weight, value_weight, w_out):
    out_blocks = w_out.astype(jnp.float32).reshape(MODEL_WIDTH, N_TP, QUERY_HEADS * HEAD_SIZE // N_TP)

    def run_group(group_pair):
        return one_group(group_pair[0], group_pair[1], norm_gain, query_gain, key_norm_gain, w_query, key_weight, value_weight, out_blocks)
    result = lax.map(run_group, (states.reshape(N_GRP, TOK_GRP, MODEL_WIDTH), lengths.reshape(N_GRP, GROUP_PROMPTS)))
    return result.reshape(TOKENS, MODEL_WIDTH)
```

```python
import functools
import math

import jax
import jax.numpy as jnp
from jax import lax
from jax.experimental import pallas as pl
from jax.experimental.pallas import tpu as pltpu
from jax.sharding import Mesh, PartitionSpec as P

AXES = ("z", "xh", "y", "xl", "c")
SIZES = (4, 2, 4, 2, 2)
X = ("xh", "xl")


def shift(value, axis, steps, size=4):
    return lax.ppermute(value, axis, [(i, (i + steps) % size) for i in range(size)])


def norm_kernel(place, x_ref, gain_ref, o_ref):
    z, y = place[0], place[1]
    x = x_ref[...].astype(jnp.float32)
    scale = lax.rsqrt(jnp.mean(x * x, axis=-1, keepdims=True) + 1e-06)
    width = x.shape[1] // 8
    piece = width // 4
    for block in range(8):
        part = x[:, block * width : (block + 1) * width]
        part = part * scale * gain_ref[:, block * width : (block + 1) * width]
        part = pltpu.roll(part, lax.rem(4 - y, 4) * piece, 1)
        target = lax.rem(block // 2 - z + 4, 4) * 2 + block % 2
        o_ref[:, pl.ds(pl.multiple_of(target * width, 128), width)] = part.astype(jnp.bfloat16)


def rolled_norm(states, gain, z, y):
    rows, width = states.shape
    step = 64
    return pl.pallas_call(
        norm_kernel,
        out_shape=jax.ShapeDtypeStruct((rows, width), jnp.bfloat16),
        grid_spec=pltpu.PrefetchScalarGridSpec(
            num_scalar_prefetch=1,
            grid=(rows // step,),
            in_specs=[
                pl.BlockSpec((step, width), lambda i, p: (i, 0)),
                pl.BlockSpec((1, width), lambda i, p: (0, 0)),
            ],
            out_specs=pl.BlockSpec((step, width), lambda i, p: (i, 0)),
        ),
        compiler_params=pltpu.CompilerParams(vmem_limit_bytes=32 * 1024 * 1024),
        cost_estimate=pl.CostEstimate(flops=rows * width * 6, bytes_accessed=rows * width * 4, transcendentals=rows),
        name="norm",
    )(jnp.stack([z, y]).astype(jnp.int32), states, gain.reshape(1, width))


def per_head_norm(vectors, scale_gain):
    return (
        vectors
        * lax.rsqrt(jnp.mean(vectors * vectors, axis=-1, keepdims=True) + 1e-06)
        * scale_gain
    )


def apply_rotary(vectors):
    head_width = vectors.shape[-1]
    half_width = head_width // 2
    freq_index = jnp.arange(half_width, dtype=jnp.float32)
    frequency = jnp.exp(freq_index * (-2.0 * math.log(1000000.0) / head_width))
    positions = jnp.arange(vectors.shape[1], dtype=jnp.float32)
    angles = positions[:, None] * frequency[None, :]
    cosine_table = jnp.cos(angles)[:, None, :]
    sine_table = jnp.sin(angles)[:, None, :]
    lower_half = vectors[..., :half_width]
    upper_half = vectors[..., half_width:]
    return jnp.concatenate(
        [
            lower_half * cosine_table - upper_half * sine_table,
            upper_half * cosine_table + lower_half * sine_table,
        ],
        axis=-1,
    )


def attend(query_heads, key_heads, value_heads, group_lengths):
    head_width = query_heads.shape[-1]
    slot_length = query_heads.shape[1]
    scores = jnp.einsum(
        "pqgrd,pkgd->pgrqk", query_heads, key_heads, preferred_element_type=jnp.float32
    ) / math.sqrt(head_width)
    positions = jnp.arange(slot_length, dtype=jnp.int32)
    causal = (positions[None, :] <= positions[:, None])[None, :, :]
    live = positions[None, None, :] < group_lengths[:, None, None]
    allowed = (causal & live)[:, None, None, :, :]
    weights = jnp.where(allowed, jnp.exp(scores), 0.0)
    probabilities = (weights / jnp.sum(weights, axis=-1, keepdims=True)).astype(jnp.bfloat16)
    return jnp.einsum(
        "pgrqk,pkgd->pqgrd", probabilities, value_heads, preferred_element_type=jnp.float32
    ).astype(jnp.bfloat16)


def first_hop(block, axis):
    return [block, shift(block, axis, -1), shift(block, axis, 2), shift(block, axis, 1)]


def second_hop(block, axis):
    after, before = shift(block, axis, -1), shift(block, axis, 1)
    half = block.shape[0] // 2
    far = [shift(after[:half], axis, -1), shift(before[half:], axis, 1)]
    return [block, after, jnp.concatenate(far, axis=0), before]


def per_device(
    states, norm_gain, query_gain, key_norm_gain, lengths, w_query, key_weight, value_weight, w_out
):
    z, y, xh, xl, c = (lax.axis_index(a) for a in ("z", "y", "xh", "xl", "c"))
    rows, width = states.shape
    piece = w_query.shape[0]
    head_width = query_gain.shape[0]
    heads_local = w_query.shape[1] // head_width
    half_rows = rows // 2

    out_full = lax.all_gather(w_out, ("z", "xh", "y"), axis=0, tiled=True)

    w_local = jnp.concatenate([w_query, key_weight, value_weight], axis=1)
    w_other = shift(w_local, "xh", 1, 2)
    w_pair = lax.dynamic_slice_in_dim(
        jnp.concatenate([w_local, w_other, w_local], axis=0), xh * piece, 2 * piece, axis=0
    )
    half = w_local.shape[1] // 2
    first, second = w_pair[:, :half], w_pair[:, half:]

    normed = rolled_norm(states, norm_gain, z, y)
    from_left = shift(normed[half_rows:], X, 1)
    from_right = shift(normed[:half_rows], X, -1)
    other_lengths = shift(lengths, "xh", 1, 2)
    mine = jnp.concatenate([normed, from_left, from_right], axis=0)
    all_rows = jnp.concatenate(
        [mine, shift(normed, "c", 1, 2), shift(mine[rows:], "c", 1, 2)], axis=0
    )

    along_y = first_hop(first, "y")
    first_block = jnp.concatenate([b[:piece] for b in along_y] + [b[piece:] for b in along_y], axis=0)
    second_block = jnp.concatenate(first_hop(second, "z"), axis=0)
    first_parts = second_hop(first_block, "z")
    second_parts = second_hop(second_block, "y")
    depth = first_block.shape[0]
    first_result = sum(
        jnp.dot(all_rows[:, i * depth : (i + 1) * depth], part, preferred_element_type=jnp.float32)
        for i, part in enumerate(first_parts)
    )
    second_weights = jnp.stack(
        [p.reshape(8, piece, half) for p in second_parts], axis=1
    ).reshape(width, half)
    second_result = jnp.dot(all_rows, second_weights, preferred_element_type=jnp.float32)

    total = all_rows.shape[0]
    slots = 32
    prompts = total // slots
    first_heads = half // head_width
    queries = jnp.concatenate(
        [first_result, second_result[:, : heads_local * head_width - half]], axis=1
    )
    key_rows = second_result[:, heads_local * head_width - half :][:, :head_width]
    value_rows = second_result[:, heads_local * head_width - half :][:, head_width:].astype(jnp.bfloat16)

    per = rows // slots
    hp = per // 2

    def prompt_lengths(core):
        own = lax.dynamic_slice_in_dim(lengths, (xl * 2 + core) * per, per)
        near = lax.dynamic_slice_in_dim(lengths, ((1 - xl) * 2 + core) * per, per)
        away = lax.dynamic_slice_in_dim(other_lengths, ((1 - xl) * 2 + core) * per, per)
        left = jnp.where(xl == 1, near, away)[hp:]
        right = jnp.where(xl == 0, near, away)[:hp]
        return [own, left, right]

    row_lengths = jnp.concatenate(prompt_lengths(c) + prompt_lengths(1 - c))

    query_heads = apply_rotary(
        per_head_norm(queries.reshape(prompts, slots, heads_local, head_width), query_gain)
    ).astype(jnp.bfloat16)
    query_heads = query_heads.reshape(prompts, slots, 1, heads_local, head_width)
    key_heads = apply_rotary(
        per_head_norm(key_rows.reshape(prompts, slots, 1, head_width), key_norm_gain)
    ).astype(jnp.bfloat16)
    value_heads = value_rows.reshape(prompts, slots, 1, head_width)
    attended = attend(query_heads, key_heads, value_heads, row_lengths).reshape(
        total, heads_local * head_width
    )

    contract = (((1,), (1,)), ((), ()))
    chunks = 4
    size = width // chunks
    outs = []
    for i in range(chunks):
        partial = lax.dot_general(
            attended, out_full[i * size : (i + 1) * size], contract, preferred_element_type=jnp.float32
        ).astype(jnp.bfloat16)
        received = shift(partial[total // 2 :], "c", 1, 2)
        chip = partial[: total // 2].astype(jnp.float32) + received.astype(jnp.float32)
        back = chip[rows:].astype(jnp.bfloat16)
        right = shift(back[:half_rows], X, -1)
        left = shift(back[half_rows:], X, 1)
        outs.append(
            (chip[:rows] + jnp.concatenate([left, right], axis=0).astype(jnp.float32)).astype(jnp.bfloat16)
        )
    return jnp.concatenate(outs, axis=1)


def solution(mesh):
    fine = Mesh(mesh.devices.reshape(SIZES), AXES)
    grp, tp = ("z", "xh", "y"), ("xl", "c")
    placed = (
        P(grp + tp, None),
        P(),
        P(),
        P(),
        P(grp),
        P(grp, tp),
        P(grp, tp),
        P(grp, tp),
        P(grp, tp),
    )
    return jax.shard_map(
        per_device, mesh=fine, in_specs=placed, out_specs=P(grp + tp, None), check_vma=False
    )
```

```python
import functools
import math

import jax
import jax.numpy as jnp
from jax import lax
from jax.experimental import pallas as pl
from jax.experimental.pallas import tpu as pltpu
from jax.sharding import Mesh, PartitionSpec as P

AXES = ("z", "xh", "y", "xl", "c")
SIZES = (4, 2, 4, 2, 2)
X = ("xh", "xl")


def shift(value, axis, steps, size=4):
    return lax.ppermute(value, axis, [(i, (i + steps) % size) for i in range(size)])


def norm_kernel(place, x_ref, gain_ref, o_ref):
    z, y = place[0], place[1]
    x = x_ref[...].astype(jnp.float32)
    scale = lax.rsqrt(jnp.mean(x * x, axis=-1, keepdims=True) + 1e-06)
    width = x.shape[1] // 8
    piece = width // 4
    for block in range(8):
        part = x[:, block * width : (block + 1) * width]
        part = part * scale * gain_ref[:, block * width : (block + 1) * width]
        part = pltpu.roll(part, lax.rem(4 - y, 4) * piece, 1)
        target = lax.rem(block // 2 - z + 4, 4) * 2 + block % 2
        o_ref[:, pl.ds(pl.multiple_of(target * width, 128), width)] = part.astype(jnp.bfloat16)


def rolled_norm(states, gain, z, y):
    rows, width = states.shape
    step = 64
    return pl.pallas_call(
        norm_kernel,
        out_shape=jax.ShapeDtypeStruct((rows, width), jnp.bfloat16),
        grid_spec=pltpu.PrefetchScalarGridSpec(
            num_scalar_prefetch=1,
            grid=(rows // step,),
            in_specs=[
                pl.BlockSpec((step, width), lambda i, p: (i, 0)),
                pl.BlockSpec((1, width), lambda i, p: (0, 0)),
            ],
            out_specs=pl.BlockSpec((step, width), lambda i, p: (i, 0)),
        ),
        compiler_params=pltpu.CompilerParams(vmem_limit_bytes=32 * 1024 * 1024),
        cost_estimate=pl.CostEstimate(flops=rows * width * 6, bytes_accessed=rows * width * 4, transcendentals=rows),
        name="norm",
    )(jnp.stack([z, y]).astype(jnp.int32), states, gain.reshape(1, width))


def attend_kernel(splits, live_ref, qgain_ref, kgain_ref, cos_ref, sin_ref, *refs):
    parts, o_ref = refs[:-1], refs[-1]
    heads = []
    for ref, count in zip(parts, splits):
        heads += [ref[:, i * 128 : (i + 1) * 128] for i in range(count)]
    rows = o_ref.shape[0]
    cosine, sine = cos_ref[...], sin_ref[...]

    def prepare(v, gain):
        v = v * lax.rsqrt(jnp.mean(v * v, axis=-1, keepdims=True) + 1e-06) * gain
        return (v * cosine + pltpu.roll(v, 64, 1) * sine).astype(jnp.bfloat16)

    count = len(heads) - 2
    queries = jnp.concatenate([prepare(h, qgain_ref[...]) for h in heads[:count]], axis=0)
    keys = prepare(heads[count], kgain_ref[...])
    values = heads[count + 1].astype(jnp.bfloat16)
    scores = lax.dot_general(
        queries, keys, (((1,), (1,)), ((), ())), preferred_element_type=jnp.float32
    ) * (1.0 / math.sqrt(128.0))
    i = lax.broadcasted_iota(jnp.int32, (rows, rows), 0)
    j = lax.broadcasted_iota(jnp.int32, (rows, rows), 1)
    allowed = (j <= i) & (j >= (i & ~31)) & (live_ref[0] > 0)
    outs = []
    for h in range(count):
        weights = jnp.where(allowed, jnp.exp(scores[h * rows : (h + 1) * rows]), 0.0)
        outs.append((weights / jnp.sum(weights, axis=-1, keepdims=True)).astype(jnp.bfloat16))
    attended = jnp.dot(jnp.concatenate(outs, axis=0), values, preferred_element_type=jnp.float32)
    for h in range(count):
        o_ref[:, h * 128 : (h + 1) * 128] = attended[h * rows : (h + 1) * rows].astype(jnp.bfloat16)


def attend(parts, row_lengths, query_gain, key_norm_gain):
    total, head_width = parts[0].shape[0], query_gain.shape[0]
    slots, step = 32, 128
    splits = [p.shape[1] // head_width for p in parts]
    count = sum(splits) - 2
    half_width = head_width // 2
    freq_index = jnp.arange(half_width, dtype=jnp.float32)
    frequency = jnp.exp(freq_index * (-2.0 * math.log(1000000.0) / head_width))
    angles = jnp.arange(slots, dtype=jnp.float32)[:, None] * frequency[None, :]
    cosine, sine = jnp.cos(angles), jnp.sin(angles)
    cosine = jnp.tile(jnp.concatenate([cosine, cosine], axis=1), (step // slots, 1))
    sine = jnp.tile(jnp.concatenate([-sine, sine], axis=1), (step // slots, 1))
    live = (jnp.arange(slots, dtype=jnp.int32)[None, :] < row_lengths[:, None]).astype(jnp.int32)
    live = live.reshape(total // step, 1, step)
    whole = lambda shape: pl.BlockSpec(shape, lambda i: (0,) * len(shape))
    return pl.pallas_call(
        functools.partial(attend_kernel, splits),
        out_shape=jax.ShapeDtypeStruct((total, count * head_width), jnp.bfloat16),
        grid=(total // step,),
        in_specs=[
            pl.BlockSpec((1, 1, step), lambda i: (i, 0, 0)),
            whole((1, head_width)),
            whole((1, head_width)),
            whole((step, head_width)),
            whole((step, head_width)),
        ]
        + [pl.BlockSpec((step, p.shape[1]), lambda i: (i, 0)) for p in parts],
        out_specs=pl.BlockSpec((step, count * head_width), lambda i: (i, 0)),
        compiler_params=pltpu.CompilerParams(vmem_limit_bytes=40 * 1024 * 1024),
        cost_estimate=pl.CostEstimate(
            flops=4 * total * step * count * head_width,
            bytes_accessed=total * count * head_width * 8,
            transcendentals=total * step * count,
        ),
        name="attend",
    )(live, query_gain.reshape(1, -1), key_norm_gain.reshape(1, -1), cosine, sine, *parts)


def first_hop(block, axis):
    return [block, shift(block, axis, -1), shift(block, axis, 2), shift(block, axis, 1)]


def second_hop(block, axis):
    after, before = shift(block, axis, -1), shift(block, axis, 1)
    half = block.shape[0] // 2
    far = [shift(after[:half], axis, -1), shift(before[half:], axis, 1)]
    return [block, after, jnp.concatenate(far, axis=0), before]


def per_device(
    states, norm_gain, query_gain, key_norm_gain, lengths, w_query, key_weight, value_weight, w_out
):
    z, y, xh, xl, c = (lax.axis_index(a) for a in ("z", "y", "xh", "xl", "c"))
    rows, width = states.shape
    piece = w_query.shape[0]
    half_rows = rows // 2

    out_full = lax.all_gather(w_out, ("z", "xh", "y"), axis=0, tiled=True)

    w_local = jnp.concatenate([w_query, key_weight, value_weight], axis=1)
    w_other = shift(w_local, "xh", 1, 2)
    w_pair = lax.dynamic_slice_in_dim(
        jnp.concatenate([w_local, w_other, w_local], axis=0), xh * piece, 2 * piece, axis=0
    )
    half = w_local.shape[1] // 2
    first, second = w_pair[:, :half], w_pair[:, half:]

    normed = rolled_norm(states, norm_gain, z, y)
    from_left = shift(normed[half_rows:], X, 1)
    from_right = shift(normed[:half_rows], X, -1)
    other_lengths = shift(lengths, "xh", 1, 2)
    mine = jnp.concatenate([normed, from_left, from_right], axis=0)
    all_rows = jnp.concatenate([mine, shift(mine, "c", 1, 2)], axis=0)

    along_y = first_hop(first, "y")
    first_block = jnp.concatenate([b[:piece] for b in along_y] + [b[piece:] for b in along_y], axis=0)
    second_block = jnp.concatenate(first_hop(second, "z"), axis=0)
    first_parts = second_hop(first_block, "z")
    second_parts = second_hop(second_block, "y")
    depth = first_block.shape[0]
    first_result = sum(
        jnp.dot(all_rows[:, i * depth : (i + 1) * depth], part, preferred_element_type=jnp.float32)
        for i, part in enumerate(first_parts)
    )
    second_weights = jnp.stack(
        [p.reshape(8, piece, half) for p in second_parts], axis=1
    ).reshape(width, half)
    second_result = jnp.dot(all_rows, second_weights, preferred_element_type=jnp.float32)

    total = all_rows.shape[0]
    slots = 32
    per = rows // slots
    hp = per // 2

    def prompt_lengths(core):
        own = lax.dynamic_slice_in_dim(lengths, (xl * 2 + core) * per, per)
        near = lax.dynamic_slice_in_dim(lengths, ((1 - xl) * 2 + core) * per, per)
        away = lax.dynamic_slice_in_dim(other_lengths, ((1 - xl) * 2 + core) * per, per)
        left = jnp.where(xl == 1, near, away)[hp:]
        right = jnp.where(xl == 0, near, away)[:hp]
        return [own, left, right]

    row_lengths = jnp.concatenate(prompt_lengths(c) + prompt_lengths(1 - c))

    attended = attend([first_result, second_result], row_lengths, query_gain, key_norm_gain)

    contract = (((1,), (1,)), ((), ()))
    chunks = 4
    size = width // chunks
    outs = []
    for i in range(chunks):
        partial = lax.dot_general(
            attended, out_full[i * size : (i + 1) * size], contract, preferred_element_type=jnp.float32
        ).astype(jnp.bfloat16)
        received = shift(partial[total // 2 :], "c", 1, 2)
        chip = partial[: total // 2].astype(jnp.float32) + received.astype(jnp.float32)
        back = chip[rows:].astype(jnp.bfloat16)
        right = shift(back[:half_rows], X, -1)
        left = shift(back[half_rows:], X, 1)
        outs.append(
            (chip[:rows] + jnp.concatenate([left, right], axis=0).astype(jnp.float32)).astype(jnp.bfloat16)
        )
    return jnp.concatenate(outs, axis=1)


def solution(mesh):
    fine = Mesh(mesh.devices.reshape(SIZES), AXES)
    grp, tp = ("z", "xh", "y"), ("xl", "c")
    placed = (
        P(grp + tp, None),
        P(),
        P(),
        P(),
        P(grp),
        P(grp, tp),
        P(grp, tp),
        P(grp, tp),
        P(grp, tp),
    )
    return jax.shard_map(
        per_device, mesh=fine, in_specs=placed, out_specs=P(grp + tp, None), check_vma=False
    )
```

```python
import functools
import math

import jax
import jax.numpy as jnp
from jax import lax
from jax.experimental import pallas as pl
from jax.experimental.pallas import tpu as pltpu
from jax.sharding import Mesh, PartitionSpec as P

AXES = ("z", "xh", "y", "xl", "c")
SIZES = (4, 2, 4, 2, 2)
X = ("xh", "xl")
MIB = 1024 * 1024


def shift(value, axis, steps, size=4):
    return lax.ppermute(value, axis, [(i, (i + steps) % size) for i in range(size)])


def cross_shift(value, steps, first):
    pairs = []
    for z in range(4):
        for y in range(4):
            for c in range(2):
                along_y = (c == 0) == first
                tz, ty = (z, (y + steps) % 4) if along_y else ((z + steps) % 4, y)
                pairs.append(((z * 4 + y) * 2 + c, (tz * 4 + ty) * 2 + c))
    return lax.ppermute(value, ("z", "y", "c"), pairs)


def x_shift(value, steps):
    pairs = []
    for x in range(4):
        for c in range(2):
            pairs.append((x * 2 + c, (x + (steps if c == 0 else -steps)) % 4 * 2 + c))
    return lax.ppermute(value, X + ("c",), pairs)


def after(value, *others):
    return lax.optimization_barrier((value,) + others)[0]


def first_hop(block, move):
    return [block, move(block, -1), move(block, 2), move(block, 1)]


def norm_kernel(place, x_ref, gain_ref, left_ref, right_ref):
    z, y = place[0], place[1]
    x = x_ref[...].astype(jnp.float32)
    scale = lax.rsqrt(jnp.mean(x * x, axis=-1, keepdims=True) + 1e-06)
    width = x.shape[1] // 8
    piece = width // 4
    for block in range(8):
        part = x[:, block * width : (block + 1) * width]
        part = part * scale * gain_ref[:, block * width : (block + 1) * width]
        part = pltpu.roll(part, lax.rem(4 - y, 4) * piece, 1).astype(jnp.bfloat16)
        target = lax.rem(block // 2 - z + 4, 4) * 2 + block % 2
        at = pl.ds(pl.multiple_of(target * width, 128), width)

        @pl.when(pl.program_id(0) < 2)
        def _():
            left_ref[:, at] = part

        @pl.when(pl.program_id(0) >= 2)
        def _():
            right_ref[:, at] = part


def rolled_norm(states, gain, place):
    rows, width = states.shape
    step = 64
    return pl.pallas_call(
        norm_kernel,
        out_shape=[jax.ShapeDtypeStruct((rows // 2, width), jnp.bfloat16)] * 2,
        grid_spec=pltpu.PrefetchScalarGridSpec(
            num_scalar_prefetch=1,
            grid=(rows // step,),
            in_specs=[
                pl.BlockSpec((step, width), lambda i, p: (i, 0)),
                pl.BlockSpec((1, width), lambda i, p: (0, 0)),
            ],
            out_specs=[
                pl.BlockSpec((step, width), lambda i, p: (jnp.minimum(i, 1), 0)),
                pl.BlockSpec((step, width), lambda i, p: (jnp.maximum(i, 2) - 2, 0)),
            ],
        ),
        compiler_params=pltpu.CompilerParams(vmem_limit_bytes=32 * MIB),
        cost_estimate=pl.CostEstimate(flops=rows * width * 6, bytes_accessed=rows * width * 4, transcendentals=rows),
        name="norm",
    )(place, states, gain.reshape(1, width))


def by_core(c, first, second):
    return jnp.where(c == 0, first, second), jnp.where(c == 0, second, first)


def attend_rows(total, live, qgain, kgain, cosine, sine, o_ref):
    rows = total.shape[0]
    count = total.shape[1] // 128 - 2
    ones = jnp.ones((128, 128), jnp.bfloat16)
    stacked = jnp.concatenate([total[:, i * 128 : (i + 1) * 128] for i in range(count + 1)], axis=0)
    squares = jnp.dot((stacked * stacked).astype(jnp.bfloat16), ones, preferred_element_type=jnp.float32)
    scaled = stacked * lax.rsqrt(squares * (1.0 / 128.0) + 1e-06)
    prepared = []
    for h in range(count + 1):
        v = scaled[h * rows : (h + 1) * rows] * (qgain if h < count else kgain)
        prepared.append((v * cosine + pltpu.roll(v, 64, 1) * sine).astype(jnp.bfloat16))
    queries = jnp.concatenate(prepared[:count], axis=0)
    values = jnp.concatenate([total[:, (count + 1) * 128 :].astype(jnp.bfloat16), ones], axis=1)
    scores = lax.dot_general(
        queries, prepared[count], (((1,), (1,)), ((), ())), preferred_element_type=jnp.float32
    )
    i = lax.broadcasted_iota(jnp.int32, (rows, rows), 0)
    j = lax.broadcasted_iota(jnp.int32, (rows, rows), 1)
    allowed = (j <= i) & (j >= (i & ~31)) & (live > 0)
    weights = [
        jnp.where(allowed, jnp.exp(scores[h * rows : (h + 1) * rows] * (1.0 / math.sqrt(128.0))), 0.0)
        for h in range(count)
    ]
    weights = jnp.concatenate(weights, axis=0).astype(jnp.bfloat16)
    attended = jnp.dot(weights, values, preferred_element_type=jnp.float32)
    for h in range(count):
        part = attended[h * rows : (h + 1) * rows]
        o_ref[:, h * 128 : (h + 1) * 128] = (part[:, :128] / part[:, 128:]).astype(jnp.bfloat16)


def qkv_kernel(place, *refs):
    x_refs, (b0, b1, b2a, b2b, b3) = refs[:8], refs[8:13]
    rest_ref, live_ref, qgain_ref, kgain_ref, cos_ref, sin_ref, o_ref, w_ref, acc_ref, sems = refs[13:]
    y, core = place[1], place[2]
    step = pl.program_id(0)
    piece = b0.shape[0] // 8
    depth = piece * 8
    columns = b0.shape[1]

    def block(index, start):
        if index == 2:
            far = b2a.shape[0]
            return b2a.at[pl.ds(start, piece)] if start < far else b2b.at[pl.ds(start - far, piece)]
        return (b0, b1, None, b3)[index].at[pl.ds(start, piece)]

    def fetch(d, pick):
        for h in range(2):
            for e in range(4):
                target = w_ref.at[pl.ds(((d * 2 + h) * 4 + e) * piece, piece)]
                pltpu.make_async_copy(pick(h, e), target, sems.at[d]).start()

    for d in range(4):
        due = step == max(d - 1, 0)

        @pl.when(due & (core == 0))
        def _():
            fetch(d, lambda h, e: block(d, (e * 2 + h) * piece))

        @pl.when(due & (core != 0))
        def _():
            fetch(d, lambda h, e: block(e, (d * 2 + h) * piece))

    @pl.when(step == 0)
    def _():
        acc_ref[...] = jnp.zeros_like(acc_ref)

    @pl.when(step < 4)
    def _():
        at = pl.ds(pl.multiple_of(step * depth, 128), depth)
        pltpu.make_async_copy(w_ref.at[at], w_ref.at[at], sems.at[step]).wait()
        rest = jnp.concatenate(
            [
                rest_ref[pl.ds(pl.multiple_of((h * 4 + lax.rem(e + y, 4)) * piece, 32), piece), :]
                for h in range(2)
                for e in range(4)
            ],
            axis=0,
        )
        for g in range(2):
            x = jnp.concatenate([r[...] for r in x_refs[g * 4 : g * 4 + 4]], axis=0)
            rows = slice(g * 512, (g + 1) * 512)
            acc_ref[rows, :columns] += jnp.dot(x, w_ref[at, :], preferred_element_type=jnp.float32)
            acc_ref[rows, columns:] += jnp.dot(x, rest, preferred_element_type=jnp.float32)

    @pl.when(step >= 4)
    def _():
        attend_rows(
            acc_ref[pl.ds(pl.multiple_of((step - 4) * 128, 128), 128), :],
            live_ref[0],
            qgain_ref[...],
            kgain_ref[...],
            cos_ref[...],
            sin_ref[...],
            o_ref,
        )


def qkv_attend(place, tokens, blocks, rest, row_lengths, query_gain, key_norm_gain):
    sub, width = tokens[0].shape
    total = sub * len(tokens)
    head_width = query_gain.shape[0]
    slots = 32
    heads_width = blocks[0].shape[1]
    columns = heads_width + rest.shape[1]
    depth = width // 4
    half_width = head_width // 2
    freq_index = jnp.arange(half_width, dtype=jnp.float32)
    frequency = jnp.exp(freq_index * (-2.0 * math.log(1000000.0) / head_width))
    angles = jnp.arange(slots, dtype=jnp.float32)[:, None] * frequency[None, :]
    cosine, sine = jnp.cos(angles), jnp.sin(angles)
    cosine = jnp.tile(jnp.concatenate([cosine, cosine], axis=1), (sub // slots, 1))
    sine = jnp.tile(jnp.concatenate([-sine, sine], axis=1), (sub // slots, 1))
    live = (jnp.arange(slots, dtype=jnp.int32)[None, :] < row_lengths[:, None]).astype(jnp.int32)
    live = live.reshape(total // sub, 1, sub)

    def rest_index(i, p):
        return lax.rem(jnp.minimum(i, 3) + p[0], 4), 0

    fixed = [*blocks[:2], *blocks[2], blocks[3]]
    small = [query_gain.reshape(1, -1), key_norm_gain.reshape(1, -1), cosine, sine]
    return pl.pallas_call(
        qkv_kernel,
        out_shape=jax.ShapeDtypeStruct((total, heads_width), jnp.bfloat16),
        grid_spec=pltpu.PrefetchScalarGridSpec(
            num_scalar_prefetch=1,
            grid=(12,),
            in_specs=[pl.BlockSpec((sub, depth), lambda i, p: (0, jnp.minimum(i, 3)))] * len(tokens)
            + [pl.BlockSpec(memory_space=pl.ANY)] * len(fixed)
            + [pl.BlockSpec((depth, rest.shape[1]), rest_index)]
            + [pl.BlockSpec((1, 1, sub), lambda i, p: (jnp.maximum(i, 4) - 4, 0, 0))]
            + [pl.BlockSpec(a.shape, lambda i, p: (0, 0)) for a in small],
            out_specs=pl.BlockSpec((sub, heads_width), lambda i, p: (jnp.maximum(i, 4) - 4, 0)),
            scratch_shapes=[
                pltpu.VMEM((width, heads_width), jnp.bfloat16),
                pltpu.VMEM((total, columns), jnp.float32),
                pltpu.SemaphoreType.DMA((4,)),
            ],
        ),
        compiler_params=pltpu.CompilerParams(vmem_limit_bytes=44 * MIB),
        cost_estimate=pl.CostEstimate(
            flops=2 * total * width * columns, bytes_accessed=2 * (total + columns) * width, transcendentals=total * sub * 8
        ),
        name="qkv_attend",
    )(place, *tokens, *fixed, rest, live, *small)


def project(rows_ref, parts):
    weights = jnp.concatenate([p[...] for p in parts], axis=0) if len(parts) > 1 else parts[0][...]
    return lax.dot_general(
        rows_ref[...], weights, (((1,), (1,)), ((), ())), preferred_element_type=jnp.float32
    )


def give_kernel(split, rows_ref, *refs):
    parts, o_ref = refs[:-1], refs[-1]
    width = o_ref.shape[1] // 2
    o_ref[:, :width] = project(rows_ref, parts[:split]).astype(jnp.bfloat16)
    o_ref[:, width:] = project(rows_ref, parts[split:]).astype(jnp.bfloat16)


def keep_kernel(split, rows_ref, *refs):
    parts, (given_ref, own_ref, left_ref, right_ref) = refs[:-4], refs[-4:]
    width = own_ref.shape[1] // 2
    half = left_ref.shape[0]
    for at, weights in ((slice(0, width), parts[:split]), (slice(width, 2 * width), parts[split:])):
        chip = project(rows_ref, weights) + given_ref[:, at].astype(jnp.float32)
        own_ref[:, at] = chip[: 2 * half]
        left_ref[:, at] = chip[2 * half : 3 * half].astype(jnp.bfloat16)
        right_ref[:, at] = chip[3 * half :].astype(jnp.bfloat16)


def project_call(attended, even, odd, given=None):
    parts = [*even, *odd]
    rows, depth = attended.shape[0] // 2, attended.shape[1]
    width = sum(p.shape[0] for p in parts)
    keep = given is not None
    whole = lambda shape: pl.BlockSpec(shape, lambda i: (0, 0))
    out = [((rows, width), jnp.bfloat16)]
    if keep:
        out = [((rows // 2, width), jnp.float32)] + [((rows // 4, width), jnp.bfloat16)] * 2
    result = pl.pallas_call(
        functools.partial(keep_kernel if keep else give_kernel, len(even)),
        out_shape=[jax.ShapeDtypeStruct(*o) for o in out],
        grid=(1,),
        in_specs=[pl.BlockSpec((rows, depth), lambda i: (0 if keep else 1, 0))]
        + [whole(p.shape) for p in parts]
        + ([whole(given.shape)] if keep else []),
        out_specs=[whole(o[0]) for o in out],
        compiler_params=pltpu.CompilerParams(vmem_limit_bytes=32 * MIB),
        cost_estimate=pl.CostEstimate(
            flops=2 * rows * width * depth, bytes_accessed=2 * (rows + width) * depth + 2 * rows * width, transcendentals=0
        ),
        name="keep" if keep else "give",
    )(attended, *parts, *([given] if keep else []))
    return result if keep else result[0]


def finish_kernel(place, *refs):
    z, y = place[0], place[1]
    chips, firsts, seconds, o_ref = refs[0:4], refs[4:8], refs[8:12], refs[12]
    use_first = lax.rem(pl.program_id(0) + 1 + place[2], 2) == 0
    sums = []
    for chip, first, second in zip(chips, firsts, seconds):
        back = jnp.where(use_first, first[...], second[...]).astype(jnp.float32)
        sums.append(chip[...] + back)
    width = sums[0].shape[1] // 2
    piece = width // 4
    for d in range(4):
        other = jnp.concatenate(
            [sums[e][:, width + d * piece : width + (d + 1) * piece] for e in range(4)], axis=1
        )
        for h, part in enumerate((sums[d][:, :width], other)):
            part = pltpu.roll(part, y * piece, 1).astype(jnp.bfloat16)
            target = lax.rem(d + z, 4) * 2 + h
            o_ref[:, pl.ds(pl.multiple_of(target * width, 128), width)] = part


def finish(place, chips, firsts, seconds):
    rows, width = chips[0].shape
    half = rows // 2
    return pl.pallas_call(
        finish_kernel,
        out_shape=jax.ShapeDtypeStruct((rows, width * 4), jnp.bfloat16),
        grid_spec=pltpu.PrefetchScalarGridSpec(
            num_scalar_prefetch=1,
            grid=(2,),
            in_specs=[pl.BlockSpec((half, width), lambda i, p: (lax.rem(i + 1 + p[2], 2), 0))] * 4
            + [pl.BlockSpec((half, width), lambda i, p: (0, 0))] * 8,
            out_specs=pl.BlockSpec((half, width * 4), lambda i, p: (i, 0)),
        ),
        compiler_params=pltpu.CompilerParams(vmem_limit_bytes=40 * MIB),
        cost_estimate=pl.CostEstimate(flops=rows * width * 8, bytes_accessed=rows * width * 32, transcendentals=0),
        name="finish",
    )(place, *chips, *firsts, *seconds)


def per_device(
    states, norm_gain, query_gain, key_norm_gain, lengths, w_query, key_weight, value_weight, w_out
):
    z, y, xh, xl, c = (lax.axis_index(a) for a in ("z", "y", "xh", "xl", "c"))
    place = jnp.stack([z, y, c]).astype(jnp.int32)
    rows = states.shape[0]
    piece = w_query.shape[0]

    key_value = jnp.concatenate([key_weight, value_weight], axis=1)
    rest = lax.all_gather(key_value, ("z", "xh", "y"), axis=0, tiled=True)

    w_query = after(w_query, key_value)
    w_other = shift(w_query, "xh", 1, 2)
    out_other = shift(w_out, "xh", 1, 2)
    other_lengths = shift(lengths, "xh", 1, 2)
    left, right = rolled_norm(states, norm_gain, place)
    w_query, w_other, left, right = lax.optimization_barrier((w_query, w_other, left, right, other_lengths))[:4]
    w_pair = lax.dynamic_slice_in_dim(
        jnp.concatenate([w_query, w_other, w_query], axis=0), xh * piece, 2 * piece, axis=0
    )

    own = by_core(c, right, left)
    first_rows = x_shift(after(own[0], out_other), 1)
    second_rows = x_shift(after(own[1], first_rows), -1)
    mine = [*own, first_rows, second_rows]
    tokens = [*mine, *(shift(v, "c", 1, 2) for v in mine)]

    near = jnp.concatenate(first_hop(w_pair, lambda v, s: cross_shift(v, s, True)), axis=0)
    along = lambda v, s: cross_shift(v, s, False)
    before_, after_ = along(near, 1), along(near, -1)
    half = near.shape[0] // 2

    even = jnp.where(xh == 0, w_out, out_other)
    odd = jnp.where(xh == 0, out_other, w_out)
    even, odd = lax.optimization_barrier((even, odd, near))[:2]
    hops = {0: (even, odd)}
    for steps in (-1, 1, 2):
        hops[-steps % 4] = shift(even, "y", steps), shift(odd, "z", steps)
        even, odd, *_ = lax.optimization_barrier((even, odd, *hops[-steps % 4]))
    far = along(after_[:half], -1), along(before_[half:], 1)
    even_near, odd_near = (jnp.concatenate([hops[k][i] for k in range(4)], axis=0) for i in range(2))
    even_near, odd_near, rest, *far = lax.optimization_barrier((even_near, odd_near, rest, *far))
    blocks = [near, after_, tuple(far), before_]
    up_z, down_z = shift(even_near, "z", -1), shift(even_near, "z", 1)
    up_y, down_y = shift(odd_near, "y", -1), shift(odd_near, "y", 1)

    per = rows // 32
    hp = per // 2

    def prompt_lengths(core):
        own = lax.dynamic_slice_in_dim(lengths, (xl * 2 + core) * per, per)
        same = lax.dynamic_slice_in_dim(lengths, ((1 - xl) * 2 + core) * per, per)
        away = lax.dynamic_slice_in_dim(other_lengths, ((1 - xl) * 2 + core) * per, per)
        from_left = jnp.where(xl == 1, same, away)[hp:]
        from_right = jnp.where(xl == 0, same, away)[:hp]
        return [*by_core(core, own[hp:], own[:hp]), *by_core(core, from_left, from_right)]

    row_lengths = jnp.concatenate(prompt_lengths(c) + prompt_lengths(1 - c))
    attended = qkv_attend(place, tokens, blocks, rest, row_lengths, query_gain, key_norm_gain)

    up_z, down_z, up_y, down_y, attended = lax.optimization_barrier((up_z, down_z, up_y, down_y, attended))
    half = even_near.shape[0] // 2
    far_z = shift(up_z[:half], "z", -1), shift(down_z[half:], "z", 1)
    far_y = shift(up_y[:half], "y", -1), shift(down_y[half:], "y", 1)
    pieces = [((even_near,), (odd_near,)), ((up_z,), (up_y,)), (far_z, far_y), ((down_z,), (down_y,))]

    results = [None] * 4
    for k in (0, 1, 3, 2):
        given = shift(project_call(attended, *pieces[k]), "c", 1, 2)
        chip, first_back, second_back = project_call(attended, *pieces[k], given)
        results[k] = (chip, x_shift(first_back, -1), x_shift(second_back, 1))
    return finish(place, *zip(*results))


def solution(mesh):
    fine = Mesh(mesh.devices.reshape(SIZES), AXES)
    grp, tp = ("z", "xh", "y"), ("xl", "c")
    placed = (
        P(grp + tp, None),
        P(),
        P(),
        P(),
        P(grp),
        P(grp, tp),
        P(grp, tp),
        P(grp, tp),
        P(grp, tp),
    )
    return jax.shard_map(
        per_device, mesh=fine, in_specs=placed, out_specs=P(grp + tp, None), check_vma=False
    )
```

```python
import functools
import math

import jax
import jax.numpy as jnp
from jax import lax
from jax.experimental import pallas as pl
from jax.experimental.pallas import tpu as pltpu
from jax.sharding import Mesh, PartitionSpec as P

AXES = ("z", "xh", "y", "xl", "c")
SIZES = (4, 2, 4, 2, 2)
X = ("xh", "xl")
MIB = 1024 * 1024


def shift(value, axis, steps, size=4):
    return lax.ppermute(value, axis, [(i, (i + steps) % size) for i in range(size)])


def cross_shift(value, steps, first):
    pairs = []
    for z in range(4):
        for y in range(4):
            for c in range(2):
                along_y = (c == 0) == first
                tz, ty = (z, (y + steps) % 4) if along_y else ((z + steps) % 4, y)
                pairs.append(((z * 4 + y) * 2 + c, (tz * 4 + ty) * 2 + c))
    return lax.ppermute(value, ("z", "y", "c"), pairs)


def x_shift(value, steps):
    pairs = []
    for x in range(4):
        for c in range(2):
            pairs.append((x * 2 + c, (x + (steps if c == 0 else -steps)) % 4 * 2 + c))
    return lax.ppermute(value, X + ("c",), pairs)


def after(value, *others):
    return lax.optimization_barrier((value,) + others)[0]


def first_hop(block, move):
    return [block, move(block, -1), move(block, 2), move(block, 1)]


def norm_kernel(place, x_ref, gain_ref, left_ref, right_ref):
    z, y = place[0], place[1]
    x = x_ref[...].astype(jnp.float32)
    scale = lax.rsqrt(jnp.mean(x * x, axis=-1, keepdims=True) + 1e-06)
    width = x.shape[1] // 8
    piece = width // 4
    for block in range(8):
        part = x[:, block * width : (block + 1) * width]
        part = part * scale * gain_ref[:, block * width : (block + 1) * width]
        part = pltpu.roll(part, lax.rem(4 - y, 4) * piece, 1).astype(jnp.bfloat16)
        target = lax.rem(block // 2 - z + 4, 4) * 2 + block % 2
        at = pl.ds(pl.multiple_of(target * width, 128), width)

        @pl.when(pl.program_id(0) < 2)
        def _():
            left_ref[:, at] = part

        @pl.when(pl.program_id(0) >= 2)
        def _():
            right_ref[:, at] = part


def rolled_norm(states, gain, place):
    rows, width = states.shape
    step = 64
    return pl.pallas_call(
        norm_kernel,
        out_shape=[jax.ShapeDtypeStruct((rows // 2, width), jnp.bfloat16)] * 2,
        grid_spec=pltpu.PrefetchScalarGridSpec(
            num_scalar_prefetch=1,
            grid=(rows // step,),
            in_specs=[
                pl.BlockSpec((step, width), lambda i, p: (i, 0)),
                pl.BlockSpec((1, width), lambda i, p: (0, 0)),
            ],
            out_specs=[
                pl.BlockSpec((step, width), lambda i, p: (jnp.minimum(i, 1), 0)),
                pl.BlockSpec((step, width), lambda i, p: (jnp.maximum(i, 2) - 2, 0)),
            ],
        ),
        compiler_params=pltpu.CompilerParams(vmem_limit_bytes=32 * MIB),
        cost_estimate=pl.CostEstimate(flops=rows * width * 6, bytes_accessed=rows * width * 4, transcendentals=rows),
        name="norm",
    )(place, states, gain.reshape(1, width))


def by_core(c, first, second):
    return jnp.where(c == 0, first, second), jnp.where(c == 0, second, first)


def attend_rows(total, live, qgain, kgain, cosine, sine, o_ref):
    rows = total.shape[0]
    count = total.shape[1] // 128 - 2
    ones = jnp.ones((128, 128), jnp.bfloat16)
    stacked = jnp.concatenate([total[:, i * 128 : (i + 1) * 128] for i in range(count + 1)], axis=0)
    squares = jnp.dot((stacked * stacked).astype(jnp.bfloat16), ones, preferred_element_type=jnp.float32)
    scaled = stacked * lax.rsqrt(squares * (1.0 / 128.0) + 1e-06)
    prepared = []
    for h in range(count + 1):
        v = scaled[h * rows : (h + 1) * rows] * (qgain if h < count else kgain)
        prepared.append((v * cosine + pltpu.roll(v, 64, 1) * sine).astype(jnp.bfloat16))
    queries = jnp.concatenate(prepared[:count], axis=0)
    values = jnp.concatenate([total[:, (count + 1) * 128 :].astype(jnp.bfloat16), ones], axis=1)
    scores = lax.dot_general(
        queries, prepared[count], (((1,), (1,)), ((), ())), preferred_element_type=jnp.float32
    )
    i = lax.broadcasted_iota(jnp.int32, (rows, rows), 0)
    j = lax.broadcasted_iota(jnp.int32, (rows, rows), 1)
    allowed = (j <= i) & (j >= (i & ~31)) & (live > 0)
    weights = [
        jnp.where(allowed, jnp.exp(scores[h * rows : (h + 1) * rows] * (1.0 / math.sqrt(128.0))), 0.0)
        for h in range(count)
    ]
    weights = jnp.concatenate(weights, axis=0).astype(jnp.bfloat16)
    attended = jnp.dot(weights, values, preferred_element_type=jnp.float32)
    for h in range(count):
        part = attended[h * rows : (h + 1) * rows]
        o_ref[:, h * 128 : (h + 1) * 128] = (part[:, :128] / part[:, 128:]).astype(jnp.bfloat16)


def qkv_kernel(place, *refs):
    x_refs, (b0, b1, b2a, b2b, b3) = refs[:8], refs[8:13]
    live_ref, qgain_ref, kgain_ref, cos_ref, sin_ref, o_ref, w_ref, acc_ref, sems = refs[13:]
    core = place[2]
    step = pl.program_id(0)
    piece = b0.shape[0] // 8
    depth = piece * 8

    def block(index, start):
        if index == 2:
            far = b2a.shape[0]
            return b2a.at[pl.ds(start, piece)] if start < far else b2b.at[pl.ds(start - far, piece)]
        return (b0, b1, None, b3)[index].at[pl.ds(start, piece)]

    def fetch(d, pick):
        for h in range(2):
            for e in range(4):
                target = w_ref.at[pl.ds(((d * 2 + h) * 4 + e) * piece, piece)]
                pltpu.make_async_copy(pick(h, e), target, sems.at[d]).start()

    for d in range(4):
        due = step == max(d - 1, 0)

        @pl.when(due & (core == 0))
        def _():
            fetch(d, lambda h, e: block(d, (e * 2 + h) * piece))

        @pl.when(due & (core != 0))
        def _():
            fetch(d, lambda h, e: block(e, (d * 2 + h) * piece))

    @pl.when(step == 0)
    def _():
        acc_ref[...] = jnp.zeros_like(acc_ref)

    @pl.when(step < 4)
    def _():
        at = pl.ds(pl.multiple_of(step * depth, 128), depth)
        pltpu.make_async_copy(w_ref.at[at], w_ref.at[at], sems.at[step]).wait()
        for g in range(2):
            x = jnp.concatenate([r[...] for r in x_refs[g * 4 : g * 4 + 4]], axis=0)
            rows = slice(g * 512, (g + 1) * 512)
            acc_ref[rows, :] += jnp.dot(x, w_ref[at, :], preferred_element_type=jnp.float32)

    @pl.when(step >= 4)
    def _():
        attend_rows(
            acc_ref[pl.ds(pl.multiple_of((step - 4) * 128, 128), 128), :],
            live_ref[0],
            qgain_ref[...],
            kgain_ref[...],
            cos_ref[...],
            sin_ref[...],
            o_ref,
        )


def qkv_attend(place, tokens, blocks, row_lengths, query_gain, key_norm_gain):
    sub, width = tokens[0].shape
    tokens = [(t, part) for t in tokens for part in range(t.shape[0] // sub)]
    total = sub * len(tokens)
    head_width = query_gain.shape[0]
    slots = 32
    columns = blocks[0].shape[1]
    heads_width = columns - 2 * head_width
    depth = width // 4
    half_width = head_width // 2
    freq_index = jnp.arange(half_width, dtype=jnp.float32)
    frequency = jnp.exp(freq_index * (-2.0 * math.log(1000000.0) / head_width))
    angles = jnp.arange(slots, dtype=jnp.float32)[:, None] * frequency[None, :]
    cosine, sine = jnp.cos(angles), jnp.sin(angles)
    cosine = jnp.tile(jnp.concatenate([cosine, cosine], axis=1), (sub // slots, 1))
    sine = jnp.tile(jnp.concatenate([-sine, sine], axis=1), (sub // slots, 1))
    live = (jnp.arange(slots, dtype=jnp.int32)[None, :] < row_lengths[:, None]).astype(jnp.int32)
    live = live.reshape(total // sub, 1, sub)

    fixed = [*blocks[:2], *blocks[2], blocks[3]]
    small = [query_gain.reshape(1, -1), key_norm_gain.reshape(1, -1), cosine, sine]
    return pl.pallas_call(
        qkv_kernel,
        out_shape=jax.ShapeDtypeStruct((total, heads_width), jnp.bfloat16),
        grid_spec=pltpu.PrefetchScalarGridSpec(
            num_scalar_prefetch=1,
            grid=(12,),
            in_specs=[pl.BlockSpec((sub, depth), lambda i, p, part=part: (part, jnp.minimum(i, 3))) for _, part in tokens]
            + [pl.BlockSpec(memory_space=pl.ANY)] * len(fixed)
            + [pl.BlockSpec((1, 1, sub), lambda i, p: (jnp.maximum(i, 4) - 4, 0, 0))]
            + [pl.BlockSpec(a.shape, lambda i, p: (0, 0)) for a in small],
            out_specs=pl.BlockSpec((sub, heads_width), lambda i, p: (jnp.maximum(i, 4) - 4, 0)),
            scratch_shapes=[
                pltpu.VMEM((width, columns), jnp.bfloat16),
                pltpu.VMEM((total, columns), jnp.float32),
                pltpu.SemaphoreType.DMA((4,)),
            ],
        ),
        compiler_params=pltpu.CompilerParams(vmem_limit_bytes=46 * MIB),
        cost_estimate=pl.CostEstimate(
            flops=2 * total * width * columns, bytes_accessed=2 * (total + columns) * width, transcendentals=total * sub * 8
        ),
        name="qkv_attend",
    )(place, *(t for t, _ in tokens), *fixed, live, *small)


def project(rows_ref, parts):
    weights = jnp.concatenate([p[...] for p in parts], axis=0) if len(parts) > 1 else parts[0][...]
    return lax.dot_general(
        rows_ref[...], weights, (((1,), (1,)), ((), ())), preferred_element_type=jnp.float32
    )


def give_kernel(split, rows_ref, *refs):
    parts, o_ref = refs[:-1], refs[-1]
    width = o_ref.shape[1] // 2
    o_ref[:, :width] = project(rows_ref, parts[:split]).astype(jnp.bfloat16)
    o_ref[:, width:] = project(rows_ref, parts[split:]).astype(jnp.bfloat16)


def keep_kernel(split, rows_ref, *refs):
    parts, (given_ref, own_ref, left_ref, right_ref) = refs[:-4], refs[-4:]
    width = own_ref.shape[1] // 2
    half = left_ref.shape[0]
    for at, weights in ((slice(0, width), parts[:split]), (slice(width, 2 * width), parts[split:])):
        chip = project(rows_ref, weights) + given_ref[:, at].astype(jnp.float32)
        own_ref[:, at] = chip[: 2 * half]
        left_ref[:, at] = chip[2 * half : 3 * half].astype(jnp.bfloat16)
        right_ref[:, at] = chip[3 * half :].astype(jnp.bfloat16)


def project_call(attended, even, odd, given=None):
    parts = [*even, *odd]
    rows, depth = attended.shape[0] // 2, attended.shape[1]
    width = sum(p.shape[0] for p in parts)
    keep = given is not None
    whole = lambda shape: pl.BlockSpec(shape, lambda i: (0, 0))
    out = [((rows, width), jnp.bfloat16)]
    if keep:
        out = [((rows // 2, width), jnp.float32)] + [((rows // 4, width), jnp.bfloat16)] * 2
    result = pl.pallas_call(
        functools.partial(keep_kernel if keep else give_kernel, len(even)),
        out_shape=[jax.ShapeDtypeStruct(*o) for o in out],
        grid=(1,),
        in_specs=[pl.BlockSpec((rows, depth), lambda i: (0 if keep else 1, 0))]
        + [whole(p.shape) for p in parts]
        + ([whole(given.shape)] if keep else []),
        out_specs=[whole(o[0]) for o in out],
        compiler_params=pltpu.CompilerParams(vmem_limit_bytes=32 * MIB),
        cost_estimate=pl.CostEstimate(
            flops=2 * rows * width * depth, bytes_accessed=2 * (rows + width) * depth + 2 * rows * width, transcendentals=0
        ),
        name="keep" if keep else "give",
    )(attended, *parts, *([given] if keep else []))
    return result if keep else result[0]


def finish_kernel(place, *refs):
    z, y = place[0], place[1]
    chips, firsts, seconds, o_ref = refs[0:4], refs[4:8], refs[8:12], refs[12]
    use_first = lax.rem(pl.program_id(0) + 1 + place[2], 2) == 0
    sums = []
    for chip, first, second in zip(chips, firsts, seconds):
        back = jnp.where(use_first, first[...], second[...]).astype(jnp.float32)
        sums.append(chip[...] + back)
    width = sums[0].shape[1] // 2
    piece = width // 4
    for d in range(4):
        other = jnp.concatenate(
            [sums[e][:, width + d * piece : width + (d + 1) * piece] for e in range(4)], axis=1
        )
        for h, part in enumerate((sums[d][:, :width], other)):
            part = pltpu.roll(part, y * piece, 1).astype(jnp.bfloat16)
            target = lax.rem(d + z, 4) * 2 + h
            o_ref[:, pl.ds(pl.multiple_of(target * width, 128), width)] = part


def finish(place, chips, firsts, seconds):
    rows, width = chips[0].shape
    half = rows // 2
    return pl.pallas_call(
        finish_kernel,
        out_shape=jax.ShapeDtypeStruct((rows, width * 4), jnp.bfloat16),
        grid_spec=pltpu.PrefetchScalarGridSpec(
            num_scalar_prefetch=1,
            grid=(2,),
            in_specs=[pl.BlockSpec((half, width), lambda i, p: (lax.rem(i + 1 + p[2], 2), 0))] * 4
            + [pl.BlockSpec((half, width), lambda i, p: (0, 0))] * 8,
            out_specs=pl.BlockSpec((half, width * 4), lambda i, p: (i, 0)),
        ),
        compiler_params=pltpu.CompilerParams(vmem_limit_bytes=40 * MIB),
        cost_estimate=pl.CostEstimate(flops=rows * width * 8, bytes_accessed=rows * width * 32, transcendentals=0),
        name="finish",
    )(place, *chips, *firsts, *seconds)


def per_device(
    states, norm_gain, query_gain, key_norm_gain, lengths, w_query, key_weight, value_weight, w_out
):
    z, y, xh, xl, c = (lax.axis_index(a) for a in ("z", "y", "xh", "xl", "c"))
    place = jnp.stack([z, y, c]).astype(jnp.int32)
    rows = states.shape[0]
    piece = w_query.shape[0]

    weights = jnp.concatenate([w_query, key_weight, value_weight], axis=1)
    other_weights = shift(weights, "xh", 1, 2)
    out_other = shift(w_out, "xh", 1, 2)
    other_lengths = shift(lengths, "xh", 1, 2)
    left, right = rolled_norm(states, norm_gain, place)
    weights, other_weights, left, right = lax.optimization_barrier(
        (weights, other_weights, left, right, other_lengths)
    )[:4]
    w_pair = lax.dynamic_slice_in_dim(
        jnp.concatenate([weights, other_weights, weights], axis=0), xh * piece, 2 * piece, axis=0
    )

    own = by_core(c, right, left)
    first_rows = x_shift(after(own[0], out_other), 1)
    second_rows = x_shift(after(own[1], first_rows), -1)
    mine = [*own, first_rows, second_rows]
    tokens = [*mine, *(shift(v, "c", 1, 2) for v in mine)]

    near = jnp.concatenate(first_hop(w_pair, lambda v, s: cross_shift(v, s, True)), axis=0)
    along = lambda v, s: cross_shift(v, s, False)
    before_, after_ = along(near, 1), along(near, -1)
    half = near.shape[0] // 2

    even = jnp.where(xh == 0, w_out, out_other)
    odd = jnp.where(xh == 0, out_other, w_out)
    even, odd = lax.optimization_barrier((even, odd, near))[:2]
    hops = {0: (even, odd)}
    for steps in (-1, 1, 2):
        hops[-steps % 4] = shift(even, "y", steps), shift(odd, "z", steps)
        even, odd, *_ = lax.optimization_barrier((even, odd, *hops[-steps % 4]))
    after_, before_ = lax.optimization_barrier((after_, before_))
    far = along(after_[:half], -1), along(before_[half:], 1)
    even_near, odd_near = (jnp.concatenate([hops[k][i] for k in range(4)], axis=0) for i in range(2))
    even_near, odd_near, *far = lax.optimization_barrier((even_near, odd_near, *far))
    blocks = [near, after_, tuple(far), before_]
    up_z, down_z = shift(even_near, "z", -1), shift(even_near, "z", 1)
    up_y, down_y = shift(odd_near, "y", -1), shift(odd_near, "y", 1)

    per = rows // 32
    hp = per // 2

    def prompt_lengths(core):
        own = lax.dynamic_slice_in_dim(lengths, (xl * 2 + core) * per, per)
        same = lax.dynamic_slice_in_dim(lengths, ((1 - xl) * 2 + core) * per, per)
        away = lax.dynamic_slice_in_dim(other_lengths, ((1 - xl) * 2 + core) * per, per)
        from_left = jnp.where(xl == 1, same, away)[hp:]
        from_right = jnp.where(xl == 0, same, away)[:hp]
        return [*by_core(core, own[hp:], own[:hp]), *by_core(core, from_left, from_right)]

    row_lengths = jnp.concatenate(prompt_lengths(c) + prompt_lengths(1 - c))
    attended = qkv_attend(place, tokens, blocks, row_lengths, query_gain, key_norm_gain)

    up_z, down_z, up_y, down_y, attended = lax.optimization_barrier((up_z, down_z, up_y, down_y, attended))
    half = even_near.shape[0] // 2
    far_z = shift(up_z[:half], "z", -1), shift(down_z[half:], "z", 1)
    far_y = shift(up_y[:half], "y", -1), shift(down_y[half:], "y", 1)
    pieces = [((even_near,), (odd_near,)), ((up_z,), (up_y,)), (far_z, far_y), ((down_z,), (down_y,))]

    results = [None] * 4
    for k in (0, 1, 3, 2):
        given = shift(project_call(attended, *pieces[k]), "c", 1, 2)
        chip, first_back, second_back = project_call(attended, *pieces[k], given)
        results[k] = (chip, x_shift(first_back, -1), x_shift(second_back, 1))
    return finish(place, *zip(*results))


def solution(mesh):
    fine = Mesh(mesh.devices.reshape(SIZES), AXES)
    grp, tp = ("z", "xh", "y"), ("xl", "c")
    placed = (
        P(grp + tp, None),
        P(),
        P(),
        P(),
        P(grp),
        P(grp, tp),
        P(grp, tp),
        P(grp, tp),
        P(grp, tp),
    )
    return jax.shard_map(
        per_device, mesh=fine, in_specs=placed, out_specs=P(grp + tp, None), check_vma=False
    )
```
